512 devices in a mesh: section: 32 (over z, core), expert: 16 (over y, x).
Axes of the slice: x: 4, y: 4, z: 16, core: 2. Of those that a mesh axis runs over, the one named last changes fastest.
Arguments:
- held: bfloat16 [32, 3072, 2048], P('section', 'expert'), may hold values from -6 to 6
- entering: bfloat16 [3072, 2048], P('expert'), may hold values from -6 to 6
- norm_gain: bfloat16 [32, 2048], P('section'), may hold values from 0.099609375 to 1.8984375
- router: bfloat16 [32, 2048, 4], P('section'), may hold values from -0.046875 to 0.046875
- w_gate: bfloat16 [32, 2048, 4096], P('section', None, 'expert'), may hold values from -0.125 to 0.125
- w_up: bfloat16 [32, 2048, 4096], P('section', None, 'expert'), may hold values from -0.125 to 0.125
- w_down: bfloat16 [32, 4096, 2048], P('section', 'expert'), may hold values from -0.375 to 0.375
- expert_ids: int32 [32, 3072, 1], P('section', 'expert'), may hold values from 0 to 3; in each aligned block of 192 rows (0 to 191, 192 to 383, ..., all dimensions but the last counted through in order) at most 72 rows name the same one
Outputs:
- mixed: bfloat16 [32, 3072, 2048], P('section', 'expert')
The draws below stay inside these ranges and needn't reach their ends.
Inputs may be any that keep to these rules, and one draw needn't show every extreme that they name: `expert_ids`: among the 192 tokens of one device at one layer, no expert is chosen more than 72 times, a bound that some block reaches.
All inputs are finite; a program needn't handle non-finite values.
Results may differ from the reference program's by a relative error of at most 0.0055.
Values may be sent and summed in bfloat16 or wider, within the bound.
No kernel may reach another device: no remote copies, remote signals or barrier semaphores. Data moves between devices by JAX's collectives and lax.ppermute only.
A program may use at most 64 MiB of HBM per device.

```python
import math
import jax
import jax.numpy as jnp
import numpy as np
from jax import lax

D = 2048
EW = 1024
EXPERTS = 4
TOK_DEV = 192
CAP = 72
TOKENS = 3072
LAYERS = 32
N_EXPERT = 16


def block_scale(own_key, shape, shards, least, top_value):
    gain, own = 1.0, jax.random.fold_in(own_key, 6)
    for dim, parts in shards:
        heights = jnp.exp(jax.random.uniform(jax.random.fold_in(own, dim), (parts,), jnp.float32, least / len(shards), top_value / len(shards)))
        gain = gain * jnp.repeat(heights, shape[dim] // parts).reshape([-1 if axis == dim else 1 for axis in range(len(shape))])
    return gain


def deal_out(rng, own, number, rows, number_of, top, reach, slope):
    sequence = jax.random.permutation(rng, number_of)
    packed, common = portions_of(number_of, rows * top, reach, slope, True), portions_of(number_of, rows * top, reach, slope, False)
    places = jnp.arange(number_of)

    def named(lengths, rotation):
        used = int((lengths > 0).sum())
        fixed = max(1, used // 4)
        passed = fixed + (places - fixed + rotation * (used - fixed)) % max(1, number_of - fixed)
        return jnp.zeros((number_of,), jnp.int32).at[sequence[jnp.where(places < fixed, places, passed)]].set(jnp.asarray(lengths, jnp.int32))

    lengths = jnp.where(number % 4 == 0, named(packed, number // 4), named(common, number - number // 4 - 1))
    mixed = jax.random.permutation(jax.random.fold_in(own, 3), number_of)
    donor, receiver = mixed[0:number_of // 2 * 2:2], mixed[1:number_of // 2 * 2:2]
    slack = jnp.minimum(lengths[donor] - 1, reach - lengths[receiver]) // 2
    slack = jnp.where((donor == sequence[0]) | (receiver == sequence[0]) | (lengths[receiver] == 0), 0, jnp.maximum(slack, 0))
    passed = jax.random.randint(jax.random.fold_in(own, 4), (number_of // 2,), 0, 1 << 20) % (slack + 1)
    lengths = lengths.at[donor].add(-passed).at[receiver].add(passed)
    items = jnp.searchsorted(jnp.cumsum(lengths), jnp.arange(rows * top), side="right").astype(jnp.int32)
    listing = items.reshape(top, rows).T
    listing = listing[jax.random.permutation(jax.random.fold_in(own, 1), rows)]
    rotation = jax.random.randint(jax.random.fold_in(own, 2), (rows, 1), 0, top)
    return jnp.take_along_axis(listing, (jnp.arange(top)[None, :] + rotation) % top, axis=1)


def portions_of(count, total, most, lean, full):
    portions = [(1 << 20) // math.isqrt(grade ** lean) + 1 for grade in range(1, count + 1)]
    largest = most if full else min(most, max(-(-total // count), total * portions[0] // sum(portions)))
    least = 1 if total - largest >= count - 1 else 0
    counts, rest = [largest] + [least] * (count - 1), total - largest - least * (count - 1)
    while rest > 0:
        movable = [i for i in range(1, count) if counts[i] < largest] or [i for i in range(1, count) if counts[i] < most]
        mass, budget = sum([portions[i] for i in movable]), rest
        for i in movable:
            addition = min(most - counts[i], max(1, budget * portions[i] // mass), rest)
            counts[i] = counts[i] + addition
            rest = rest - addition
    return np.array(counts)


def centred(own_key, dims, deviation, reach, pieces=(), kind=jnp.bfloat16):
    level = block_scale(own_key, dims, pieces, -0.22, 0.18) if pieces else 1.0
    values = jax.random.normal(own_key, dims, jnp.float32) * deviation * level
    return jnp.minimum(jnp.maximum(values, -reach), reach).astype(kind)


def setup_inputs(seed: int = 0) -> dict:
    streams_of = jax.random.split(jax.random.key(seed), 9)
    held = centred(streams_of[0], (LAYERS, TOKENS, D), 1.0, 6.0, ((0, 32), (1, 16)))
    entering = centred(streams_of[1], (TOKENS, D), 1.0, 6.0, ((0, 16),))
    norm_gain = jnp.clip(1.0 + 0.18 * jax.random.normal(streams_of[2], (LAYERS, D), jnp.float32), 0.099609375, 1.8984375).astype(jnp.bfloat16)
    router = centred(streams_of[3], (LAYERS, D, EXPERTS), (D * 8) ** -0.5, 0.046875, ((0, 32),))
    w_gate = centred(streams_of[4], (LAYERS, D, EXPERTS * EW), D ** -0.5, 0.125, ((0, 32), (2, 16)))
    w_up = centred(streams_of[5], (LAYERS, D, EXPERTS * EW), D ** -0.5, 0.125, ((0, 32), (2, 16)))
    w_down = centred(streams_of[6], (LAYERS, EXPERTS * EW, D), (EW // 4) ** -0.5, 0.375, ((0, 32), (1, 16)))
    expert_ids_keys = jax.random.split(jax.random.fold_in(streams_of[7], 1), LAYERS * TOKENS // TOK_DEV)
    expert_ids_turns = jax.random.permutation(jax.random.fold_in(streams_of[7], 3), LAYERS * TOKENS // TOK_DEV)
    expert_ids = jax.vmap(lambda own, number: deal_out(jax.random.fold_in(streams_of[7], 2), own, number, TOK_DEV, EXPERTS, 1, CAP, 2))(expert_ids_keys, expert_ids_turns).reshape((LAYERS, TOKENS, 1))
    return {"held": held, "entering": entering, "norm_gain": norm_gain, "router": router, "w_gate": w_gate, "w_up": w_up, "w_down": w_down, "expert_ids": expert_ids}


def normalize(rows_in, gain_row):
    values = rows_in.astype(jnp.float32)
    scaling = lax.rsqrt(lax.optimization_barrier(jnp.mean(values * values, axis=-1, keepdims=True)) + 1e-06)
    return (values * scaling * gain_row.astype(jnp.float32)).astype(jnp.bfloat16)

def reference(held, entering, norm_gain, router, w_gate, w_up, w_down, expert_ids):
    arriving_all = jnp.concatenate([entering[None], held[:-1]], axis=0)
    units = EXPERTS * EW // N_EXPERT
    most_rows = N_EXPERT * CAP
    highest = lax.Precision.HIGHEST

    def layer(carry, inputs):
        arriving, gain_row, router_layer, gate_layer, up_layer, down_layer, labels = inputs
        normed = normalize(arriving, gain_row)
        logits = jnp.dot(normed, router_layer, preferred_element_type=jnp.float32)
        weights = jnp.exp(logits)
        probability = weights / lax.optimization_barrier(jnp.sum(weights, axis=1, keepdims=True))
        chosen = labels[:, 0].astype(jnp.int32)
        gate_value = jnp.take_along_axis(probability, chosen[:, None], axis=1)[:, 0]
        wide = normed.astype(jnp.float32)
        mixture = jnp.zeros((TOKENS, D), jnp.float32)
        for expert in range(EXPERTS):
            matches = chosen == expert
            positions = jnp.nonzero(matches, size=most_rows, fill_value=0)[0]
            valid = (jnp.arange(most_rows) < jnp.sum(matches)).astype(jnp.float32)
            picked = wide[positions]
            low = expert * EW
            gate_proj = jnp.dot(picked, gate_layer[:, low:low + EW].astype(jnp.float32), precision=highest)
            up_proj = jnp.dot(picked, up_layer[:, low:low + EW].astype(jnp.float32), precision=highest)
            hidden = lax.optimization_barrier((jax.nn.silu(gate_proj) * up_proj).astype(jnp.bfloat16)).astype(jnp.float32)
            total = jnp.zeros((most_rows, D), jnp.float32)
            for panel in range(EW // units):
                down_rows = down_layer[low + panel * units:low + (panel + 1) * units].astype(jnp.float32)
                part = jnp.dot(hidden[:, panel * units:(panel + 1) * units], down_rows, precision=highest)
                total = total + lax.optimization_barrier(part.astype(jnp.bfloat16)).astype(jnp.float32)
            mixture = mixture.at[positions].add(total * valid[:, None])
        mixed = (arriving.astype(jnp.float32) + gate_value[:, None] * mixture).astype(jnp.bfloat16)
        return (carry, mixed)
    _, result = lax.scan(layer, jnp.float32(0.0), (arriving_all, norm_gain, router, w_gate, w_up, w_down, expert_ids))
    return result
```

```python
import jax
import jax.numpy as jnp
from jax import lax
from jax.sharding import PartitionSpec as P

CAP = 72


def passed_along(block, axis, distance):
    devices = range(lax.axis_size(axis))
    route = [(i - distance, i) for i in devices if i - distance in devices]
    return lax.ppermute(block, axis, route)


def normalize(rows_in, gain_row):
    values = rows_in.astype(jnp.float32)
    scaling = lax.rsqrt(jnp.mean(values * values, axis=-1, keepdims=True) + 1e-06)
    return (values * scaling * gain_row.astype(jnp.float32)).astype(jnp.bfloat16)


def local(held, entering, norm_gain, router, w_gate, w_up, w_down, expert_ids):
    experts = router.shape[2]
    panels = lax.axis_size("expert") // experts
    along_row = [[e * panels + p for p in range(panels)] for e in range(experts)]
    along_column = [[e * panels + p for e in range(experts)] for p in range(panels)]
    tokens, features = entering.shape
    slots = experts * CAP

    down = lax.all_gather(w_down[0], "expert", axis_index_groups=along_row, axis=0, tiled=True)

    chosen = expert_ids[0, :, 0]
    assigned = chosen[:, None] == jnp.arange(experts, dtype=jnp.int32)[None, :]
    earlier = jnp.tril(jnp.ones((tokens, tokens), jnp.bfloat16), -1)
    ranks = jnp.dot(earlier, assigned.astype(jnp.bfloat16), preferred_element_type=jnp.float32)
    place = jnp.sum(jnp.where(assigned, ranks, 0.0), axis=1).astype(jnp.int32) + chosen * CAP
    slot_index = jnp.arange(slots, dtype=jnp.int32)
    select = (place[None, :] == slot_index[:, None]).astype(jnp.bfloat16)
    spread = (place[:, None] == slot_index[None, :]).astype(jnp.bfloat16)

    arrived = passed_along(held[0], "section", 1)
    arriving = jnp.where(lax.axis_index("section") == 0, entering, arrived)
    normed = normalize(arriving, norm_gain[0])
    sent = jnp.dot(select, normed, preferred_element_type=jnp.float32).astype(jnp.bfloat16)

    mine = lax.all_to_all(
        sent, "expert", split_axis=0, concat_axis=0, axis_index_groups=along_column, tiled=True
    )
    rows = lax.all_gather(mine, "expert", axis_index_groups=along_row, axis=0, tiled=True)

    gate_proj = jnp.dot(rows, w_gate[0], preferred_element_type=jnp.float32)
    up_proj = jnp.dot(rows, w_up[0], preferred_element_type=jnp.float32)
    hidden = (jax.nn.silu(gate_proj) * up_proj).astype(jnp.bfloat16)
    own = lax.all_to_all(
        hidden, "expert", split_axis=0, concat_axis=0, axis_index_groups=along_row, tiled=True
    )
    units = hidden.shape[1]
    own = own.reshape(panels, slots, units)
    wide = own.transpose(1, 0, 2).reshape(slots, panels * units)
    total = jnp.dot(wide, down, preferred_element_type=jnp.float32).astype(jnp.bfloat16)
    returned = lax.all_to_all(
        total, "expert", split_axis=0, concat_axis=0, axis_index_groups=along_column, tiled=True
    )
    mixture = jnp.dot(spread, returned, preferred_element_type=jnp.float32)

    logits = jnp.dot(normed, router[0], preferred_element_type=jnp.float32)
    weights = jnp.exp(logits)
    probability = weights / jnp.sum(weights, axis=1, keepdims=True)
    gate_value = jnp.sum(jnp.where(assigned, probability, 0.0), axis=1)
    mixed = (arriving.astype(jnp.float32) + gate_value[:, None] * mixture).astype(jnp.bfloat16)
    return mixed[None]


def solution(mesh):
    placed = (
        P("section", "expert", None),
        P("expert", None),
        P("section", None),
        P("section", None, None),
        P("section", None, "expert"),
        P("section", None, "expert"),
        P("section", "expert", None),
        P("section", "expert", None),
    )
    return jax.shard_map(
        local, mesh=mesh, in_specs=placed, out_specs=P("section", "expert", None), check_vma=False
    )
```

```python
import jax
import jax.numpy as jnp
from jax import lax
from jax.experimental import pallas as pl
from jax.experimental.pallas import tpu as pltpu
from jax.sharding import PartitionSpec as P

CAP = 72
VMEM_BYTES = 40 * 1024 * 1024


def passed_along(block, axis, distance):
    devices = range(lax.axis_size(axis))
    route = [(i - distance, i) for i in devices if i - distance in devices]
    return lax.ppermute(block, axis, route)


def normalize(rows_in, gain_row):
    values = rows_in.astype(jnp.float32)
    scaling = lax.rsqrt(jnp.mean(values * values, axis=-1, keepdims=True) + 1e-06)
    return (values * scaling * gain_row.astype(jnp.float32)).astype(jnp.bfloat16)


def product(left, right):
    return jnp.dot(left, right, preferred_element_type=jnp.float32)


def whole(shape):
    return pl.BlockSpec(shape, lambda i: (0, 0))


def hidden_kernel(rows_ref, gate_ref, up_ref, hidden_ref):
    rows = rows_ref[...]
    gate_proj = product(rows, gate_ref[...])
    up_proj = product(rows, up_ref[...])
    hidden_ref[...] = (jax.nn.silu(gate_proj) * up_proj).astype(hidden_ref.dtype)


def hidden_units(rows, gate, up, steps=4):
    count, features = rows.shape
    units = gate.shape[1]
    block = count // steps
    return pl.pallas_call(
        hidden_kernel,
        grid=(steps,),
        out_shape=jax.ShapeDtypeStruct((count, units), jnp.bfloat16),
        in_specs=[
            pl.BlockSpec((block, features), lambda i: (i, 0)),
            whole((features, units)),
            whole((features, units)),
        ],
        out_specs=pl.BlockSpec((block, units), lambda i: (i, 0)),
        compiler_params=pltpu.CompilerParams(vmem_limit_bytes=VMEM_BYTES),
        cost_estimate=pl.CostEstimate(
            flops=4 * count * features * units,
            bytes_accessed=2 * (count * (features + units) + 2 * features * units),
            transcendentals=count * units,
        ),
    )(rows, gate, up)


def down_kernel(hidden_ref, other_ref, down_ref, down_other_ref, part_ref):
    total = product(hidden_ref[...], down_ref[...])
    total += product(other_ref[...], down_other_ref[...])
    part_ref[...] = total.astype(part_ref.dtype)


def down_part(hidden, other, down, down_other, steps=4):
    count, units = hidden.shape
    features = down.shape[1]
    block = features // steps
    return pl.pallas_call(
        down_kernel,
        grid=(steps,),
        out_shape=jax.ShapeDtypeStruct((count, features), jnp.bfloat16),
        in_specs=[
            whole((count, units)),
            whole((count, units)),
            pl.BlockSpec((units, block), lambda i: (0, i)),
            pl.BlockSpec((units, block), lambda i: (0, i)),
        ],
        out_specs=pl.BlockSpec((count, block), lambda i: (0, i)),
        compiler_params=pltpu.CompilerParams(vmem_limit_bytes=VMEM_BYTES),
        cost_estimate=pl.CostEstimate(
            flops=4 * count * features * units,
            bytes_accessed=2 * (count * (features + 2 * units) + 2 * features * units),
            transcendentals=0,
        ),
    )(hidden, other, down, down_other)


def local(held, entering, norm_gain, router, w_gate, w_up, w_down, expert_ids):
    experts = router.shape[2]
    group = lax.axis_size("expert")
    panels = group // experts
    tokens, features = entering.shape
    swap = [(i, i ^ 1) for i in range(group)]
    column_pairs = [(x, panels - 1 - x) for x in range(panels // 2)]
    token_groups = [[e * panels + x for e in range(experts) for x in pair] for pair in column_pairs]
    copies = 2
    span = copies * CAP
    slots = experts * span

    gate_other = lax.ppermute(w_gate[0], "expert", swap)
    up_other = lax.ppermute(w_up[0], "expert", swap)
    down_other = lax.ppermute(w_down[0], "expert", swap)
    arrived = passed_along(held[0], "section", 1)

    chosen = expert_ids[0, :, 0]
    assigned = chosen[:, None] == jnp.arange(experts, dtype=jnp.int32)[None, :]
    earlier = jnp.tril(jnp.ones((tokens, tokens), jnp.bfloat16), -1)
    ranks = product(earlier, assigned.astype(jnp.bfloat16))
    place = jnp.sum(jnp.where(assigned, ranks, 0.0), axis=1).astype(jnp.int32) + chosen * span
    slot_index = jnp.arange(slots, dtype=jnp.int32)
    row_slot = slot_index - jnp.where(slot_index % span < CAP, 0, CAP)
    select = (place[None, :] == row_slot[:, None]).astype(jnp.bfloat16)
    spread = (place[:, None] == row_slot[None, :]).astype(jnp.bfloat16)

    def dispatch(select, arriving):
        normed = normalize(arriving, norm_gain[0])
        sent = product(select, normed).astype(jnp.bfloat16)
        rows = lax.all_to_all(
            sent, "expert", split_axis=0, concat_axis=0, axis_index_groups=token_groups, tiled=True
        )
        return normed, rows

    def nothing(select, arriving):
        return arriving, jnp.zeros((slots, features), jnp.bfloat16)

    here = lax.axis_index("section") < lax.axis_size("section")
    arriving = jnp.where(lax.axis_index("section") == 0, entering, arrived)
    normed, rows = lax.cond(here, dispatch, nothing, select, arriving)

    hidden = hidden_units(rows, w_gate[0], w_up[0])
    hidden_other = hidden_units(rows, gate_other, up_other)
    part = down_part(hidden, hidden_other, w_down[0], down_other)
    returned = lax.all_to_all(
        part, "expert", split_axis=0, concat_axis=0, axis_index_groups=token_groups, tiled=True
    )
    mixture = product(spread, returned)

    logits = product(normed, router[0])
    weights = jnp.exp(logits)
    probability = weights / jnp.sum(weights, axis=1, keepdims=True)
    gate_value = jnp.sum(jnp.where(assigned, probability, 0.0), axis=1)
    mixed = (arriving.astype(jnp.float32) + gate_value[:, None] * mixture).astype(jnp.bfloat16)
    return mixed[None]


def solution(mesh):
    placed = (
        P("section", "expert", None),
        P("expert", None),
        P("section", None),
        P("section", None, None),
        P("section", None, "expert"),
        P("section", None, "expert"),
        P("section", "expert", None),
        P("section", "expert", None),
    )
    return jax.shard_map(
        local, mesh=mesh, in_specs=placed, out_specs=P("section", "expert", None), check_vma=False
    )
```

```python
import jax
import jax.numpy as jnp
from jax import lax
from jax.experimental import pallas as pl
from jax.experimental.pallas import tpu as pltpu
from jax.sharding import PartitionSpec as P

CAP = 72
VMEM_BYTES = 40 * 1024 * 1024


def passed_along(block, axis, distance):
    devices = range(lax.axis_size(axis))
    route = [(i - distance, i) for i in devices if i - distance in devices]
    return lax.ppermute(block, axis, route)


def normalize(rows_in, gain_row):
    values = rows_in.astype(jnp.float32)
    scaling = lax.rsqrt(jnp.mean(values * values, axis=-1, keepdims=True) + 1e-06)
    return (values * scaling * gain_row.astype(jnp.float32)).astype(jnp.bfloat16)


def product(left, right):
    return jnp.dot(left, right, preferred_element_type=jnp.float32)


def whole(shape):
    return pl.BlockSpec(shape, lambda i: (0, 0))


def hidden_kernel(rows_ref, gate_ref, up_ref, hidden_ref):
    rows = rows_ref[...]
    gate_proj = product(rows, gate_ref[...])
    up_proj = product(rows, up_ref[...])
    hidden_ref[...] = (jax.nn.silu(gate_proj) * up_proj).astype(hidden_ref.dtype)


def hidden_units(rows, gate, up, steps=4):
    count, features = rows.shape
    units = gate.shape[1]
    block = count // steps
    return pl.pallas_call(
        hidden_kernel,
        grid=(steps,),
        out_shape=jax.ShapeDtypeStruct((count, units), jnp.bfloat16),
        in_specs=[
            pl.BlockSpec((block, features), lambda i: (i, 0)),
            whole((features, units)),
            whole((features, units)),
        ],
        out_specs=pl.BlockSpec((block, units), lambda i: (i, 0)),
        compiler_params=pltpu.CompilerParams(vmem_limit_bytes=VMEM_BYTES),
        cost_estimate=pl.CostEstimate(
            flops=4 * count * features * units,
            bytes_accessed=2 * (count * (features + units) + 2 * features * units),
            transcendentals=count * units,
        ),
    )(rows, gate, up)


def down_kernel(hidden_ref, other_ref, down_ref, down_other_ref, part_ref):
    total = product(hidden_ref[...], down_ref[...])
    total += product(other_ref[...], down_other_ref[...])
    part_ref[...] = total.astype(part_ref.dtype)


def down_part(hidden, other, down, down_other, steps=4):
    count, units = hidden.shape
    features = down.shape[1]
    block = features // steps
    return pl.pallas_call(
        down_kernel,
        grid=(steps,),
        out_shape=jax.ShapeDtypeStruct((count, features), jnp.bfloat16),
        in_specs=[
            whole((count, units)),
            whole((count, units)),
            pl.BlockSpec((units, block), lambda i: (0, i)),
            pl.BlockSpec((units, block), lambda i: (0, i)),
        ],
        out_specs=pl.BlockSpec((count, block), lambda i: (0, i)),
        compiler_params=pltpu.CompilerParams(vmem_limit_bytes=VMEM_BYTES),
        cost_estimate=pl.CostEstimate(
            flops=4 * count * features * units,
            bytes_accessed=2 * (count * (features + 2 * units) + 2 * features * units),
            transcendentals=0,
        ),
    )(hidden, other, down, down_other)


def local(held, entering, norm_gain, router, w_gate, w_up, w_down, expert_ids):
    experts = router.shape[2]
    group = lax.axis_size("expert")
    panels = group // experts
    tokens, features = entering.shape
    sections = lax.axis_size("section")
    everywhere = ("section", "expert")
    near, mirrored = (lambda x: x ^ 1), (lambda x: panels - 1 - x)
    swap, token_groups = [], []
    for section in range(sections):
        weight_partner, token_partner = (near, mirrored) if section % 2 == 0 else (mirrored, near)
        start = section * group
        for i in range(group):
            swap.append((start + i, start + i - i % panels + weight_partner(i % panels)))
        for x in range(panels):
            if x < token_partner(x):
                pair = (x, token_partner(x))
                token_groups.append([start + e * panels + c for e in range(experts) for c in pair])
    copies = 2
    span = copies * CAP
    slots = experts * span

    gate_other = lax.ppermute(w_gate[0], everywhere, swap)
    up_other = lax.ppermute(w_up[0], everywhere, swap)
    down_other = lax.ppermute(w_down[0], everywhere, swap)
    arrived = passed_along(held[0], "section", 1)

    chosen = expert_ids[0, :, 0]
    assigned = chosen[:, None] == jnp.arange(experts, dtype=jnp.int32)[None, :]
    earlier = jnp.tril(jnp.ones((tokens, tokens), jnp.bfloat16), -1)
    ranks = product(earlier, assigned.astype(jnp.bfloat16))
    place = jnp.sum(jnp.where(assigned, ranks, 0.0), axis=1).astype(jnp.int32) + chosen * span
    slot_index = jnp.arange(slots, dtype=jnp.int32)
    row_slot = slot_index - jnp.where(slot_index % span < CAP, 0, CAP)
    select = (place[None, :] == row_slot[:, None]).astype(jnp.bfloat16)
    spread = (place[:, None] == row_slot[None, :]).astype(jnp.bfloat16)

    def dispatch(select, arriving):
        normed = normalize(arriving, norm_gain[0])
        sent = product(select, normed).astype(jnp.bfloat16)
        rows = lax.all_to_all(
            sent, everywhere, split_axis=0, concat_axis=0, axis_index_groups=token_groups, tiled=True
        )
        return normed, rows

    def nothing(select, arriving):
        return arriving, jnp.zeros((slots, features), jnp.bfloat16)

    here = lax.axis_index("section") < lax.axis_size("section")
    arriving = jnp.where(lax.axis_index("section") == 0, entering, arrived)
    normed, rows = lax.cond(here, dispatch, nothing, select, arriving)

    hidden = hidden_units(rows, w_gate[0], w_up[0])
    hidden_other = hidden_units(rows, gate_other, up_other)
    part = down_part(hidden, hidden_other, w_down[0], down_other)
    returned = lax.all_to_all(
        part, everywhere, split_axis=0, concat_axis=0, axis_index_groups=token_groups, tiled=True
    )
    mixture = product(spread, returned)

    logits = product(normed, router[0])
    weights = jnp.exp(logits)
    probability = weights / jnp.sum(weights, axis=1, keepdims=True)
    gate_value = jnp.sum(jnp.where(assigned, probability, 0.0), axis=1)
    mixed = (arriving.astype(jnp.float32) + gate_value[:, None] * mixture).astype(jnp.bfloat16)
    return mixed[None]


def solution(mesh):
    placed = (
        P("section", "expert", None),
        P("expert", None),
        P("section", None),
        P("section", None, None),
        P("section", None, "expert"),
        P("section", None, "expert"),
        P("section", "expert", None),
        P("section", "expert", None),
    )
    return jax.shard_map(
        local, mesh=mesh, in_specs=placed, out_specs=P("section", "expert", None), check_vma=False
    )
```

```python
import jax
import jax.numpy as jnp
from jax import lax
from jax.experimental import pallas as pl
from jax.experimental.pallas import tpu as pltpu
from jax.sharding import PartitionSpec as P

CAP = 72
VMEM_BYTES = 48 * 1024 * 1024
HIDDEN_VMEM_BYTES = 52 * 1024 * 1024


def passed_along(block, axis, distance):
    devices = range(lax.axis_size(axis))
    route = [(i - distance, i) for i in devices if i - distance in devices]
    return lax.ppermute(block, axis, route)


def product(left, right):
    return jnp.dot(left, right, preferred_element_type=jnp.float32)


def anywhere():
    return pl.BlockSpec(memory_space=pl.ANY)


def column_of(row, zero):
    size = row.shape[1]
    across, down = (lax.broadcasted_iota(jnp.int32, (size, size), d) for d in (1, 0))
    return jnp.sum(jnp.where(across == down, row, zero), axis=1, keepdims=True)


def front_kernel(first_ref, small_ref, arrived_ref, entering_ref, arriving_ref, gate_ref, place_ref, sent_ref, sent, out_sems):
    slots, features = sent.shape
    tokens = arrived_ref.shape[0]
    experts = small_ref.shape[0] - 2
    steps = out_sems.shape[0]
    block = slots // steps
    span = 2 * CAP

    router = small_ref[:experts, :].astype(jnp.bfloat16)
    gain = small_ref[experts : experts + 1, :]
    chosen = small_ref[experts + 1 :, :tokens].astype(jnp.int32)
    assigned = chosen == lax.broadcasted_iota(jnp.int32, (experts, tokens), 0)
    across, down = (lax.broadcasted_iota(jnp.int32, (tokens, tokens), d) for d in (1, 0))
    ranks = product(assigned.astype(jnp.bfloat16), (down < across).astype(jnp.bfloat16))
    rank = jnp.sum(jnp.where(assigned, ranks, 0.0), axis=0, keepdims=True).astype(jnp.int32)
    place = rank + chosen * span
    place_ref[...] = column_of(place, 0)
    slot = lax.broadcasted_iota(jnp.int32, (slots, tokens), 0)
    row_slot = jnp.where(slot % span < CAP, slot, slot - CAP)
    select = (place == row_slot).astype(jnp.bfloat16)

    arriving = jnp.where(first_ref[0] == 1, entering_ref[...], arrived_ref[...])
    arriving_ref[...] = arriving
    values = arriving.astype(jnp.float32)
    written = []
    scaling = lax.rsqrt(jnp.mean(values * values, axis=-1, keepdims=True) + 1e-06)
    normed = (values * scaling * gain).astype(jnp.bfloat16)
    for step in range(steps):
        here = pl.ds(step * block, block)
        sent[here, :] = product(select[step * block : (step + 1) * block], normed).astype(jnp.bfloat16)
        copy = pltpu.make_async_copy(sent.at[here], sent_ref.at[here], out_sems.at[step])
        copy.start()
        written.append(copy)
    logits = lax.dot_general(router, normed, (((1,), (1,)), ((), ())), preferred_element_type=jnp.float32)
    weights = jnp.exp(logits)
    probability = weights / jnp.sum(weights, axis=0, keepdims=True)
    gate_ref[...] = column_of(jnp.sum(jnp.where(assigned, probability, 0.0), axis=0, keepdims=True), 0.0)
    for copy in written:
        copy.wait()


def front(first, small, arrived, entering, slots, steps=2):
    tokens, features = entering.shape
    vmem = pl.BlockSpec(memory_space=pltpu.VMEM)
    return pl.pallas_call(
        front_kernel,
        out_shape=(
            jax.ShapeDtypeStruct((tokens, features), jnp.bfloat16),
            jax.ShapeDtypeStruct((tokens, 1), jnp.float32),
            jax.ShapeDtypeStruct((tokens, 1), jnp.int32),
            jax.ShapeDtypeStruct((slots, features), jnp.bfloat16),
        ),
        in_specs=[pl.BlockSpec(memory_space=pltpu.SMEM)] + [vmem] * 3,
        out_specs=(vmem, vmem, vmem, anywhere()),
        scratch_shapes=[
            pltpu.VMEM((slots, features), jnp.bfloat16),
            pltpu.SemaphoreType.DMA((steps,)),
        ],
        compiler_params=pltpu.CompilerParams(vmem_limit_bytes=VMEM_BYTES),
        cost_estimate=pl.CostEstimate(
            flops=40 * slots * tokens * features, bytes_accessed=2 * features * (3 * tokens + slots), transcendentals=tokens
        ),
    )(first, small, arrived, entering)


def hidden_kernel(rows_ref, gate_ref, up_ref, gate_other_ref, up_other_ref, hidden_ref, rows, gate_up, in_sems):
    count, features = rows.shape
    units = gate_ref.shape[1]
    steps = 2
    block = count // steps

    def fetch(source, target, index):
        copy = pltpu.make_async_copy(source, target, in_sems.at[index])
        copy.start()
        return copy

    first, second = pl.ds(0, units), pl.ds(units, units)
    row_copy = fetch(rows_ref, rows, 0)
    panels = [
        (fetch(gate, gate_up.at[i, :, first], 1 + 2 * i), fetch(up, gate_up.at[i, :, second], 2 + 2 * i))
        for i, (gate, up) in enumerate(((gate_ref, up_ref), (gate_other_ref, up_other_ref)))
    ]
    row_copy.wait()
    for i, copies in enumerate(panels):
        for copy in copies:
            copy.wait()

        def multiply(step, carry):
            here = pl.ds(pl.multiple_of(step * block, block), block)
            both = product(rows[here, :], gate_up[i])
            units_here = jax.nn.silu(both[:, :units]) * both[:, units:]
            hidden_ref[here, i * units : (i + 1) * units] = units_here.astype(jnp.bfloat16)
            return carry

        lax.fori_loop(0, steps, multiply, 0)


def hidden_units(rows, gate, up, gate_other, up_other):
    count, features = rows.shape
    units = gate.shape[1]
    return pl.pallas_call(
        hidden_kernel,
        out_shape=jax.ShapeDtypeStruct((count, 2 * units), jnp.bfloat16),
        in_specs=[anywhere()] * 5,
        out_specs=pl.BlockSpec(memory_space=pltpu.VMEM),
        scratch_shapes=[
            pltpu.VMEM((count, features), jnp.bfloat16),
            pltpu.VMEM((2, features, 2 * units), jnp.bfloat16),
            pltpu.SemaphoreType.DMA((5,)),
        ],
        compiler_params=pltpu.CompilerParams(vmem_limit_bytes=HIDDEN_VMEM_BYTES),
        cost_estimate=pl.CostEstimate(
            flops=8 * count * features * units,
            bytes_accessed=2 * (count * features + 4 * features * units),
            transcendentals=2 * count * units,
        ),
    )(rows, gate, up, gate_other, up_other)


def down_kernel(hidden_ref, down_ref, down_other_ref, part_ref):
    units = down_ref.shape[0]
    total = product(hidden_ref[:, :units], down_ref[...])
    total += product(hidden_ref[:, units:], down_other_ref[...])
    part_ref[...] = total.astype(part_ref.dtype)


def down_part(hidden, down, down_other, steps=4):
    count = hidden.shape[0]
    units, features = down.shape
    block = features // steps
    return pl.pallas_call(
        down_kernel,
        grid=(steps,),
        out_shape=jax.ShapeDtypeStruct((count, features), jnp.bfloat16),
        in_specs=[
            pl.BlockSpec((count, 2 * units), lambda i: (0, 0)),
            pl.BlockSpec((units, block), lambda i: (0, i)),
            pl.BlockSpec((units, block), lambda i: (0, i)),
        ],
        out_specs=pl.BlockSpec((count, block), lambda i: (0, i)),
        compiler_params=pltpu.CompilerParams(vmem_limit_bytes=VMEM_BYTES),
        cost_estimate=pl.CostEstimate(
            flops=4 * count * features * units,
            bytes_accessed=2 * (count * (features + 2 * units) + 2 * features * units),
            transcendentals=0,
        ),
    )(hidden, down, down_other)


def combine_kernel(place_ref, returned_ref, arriving_ref, gate_ref, mixed_ref):
    tokens, slots = place_ref.shape[0], returned_ref.shape[0]
    slot = lax.broadcasted_iota(jnp.int32, (tokens, slots), 1)
    row_slot = jnp.where(slot % (2 * CAP) < CAP, slot, slot - CAP)
    spread = (place_ref[...] == row_slot).astype(jnp.bfloat16)
    mixture = product(spread, returned_ref[...])
    mixed = arriving_ref[...].astype(jnp.float32) + gate_ref[...] * mixture
    mixed_ref[0] = mixed.astype(mixed_ref.dtype)


def combine(place, returned, arriving, gate_value, steps=1):
    tokens, features = arriving.shape
    slots = returned.shape[0]
    block = features // steps
    return pl.pallas_call(
        combine_kernel,
        grid=(steps,),
        out_shape=jax.ShapeDtypeStruct((1, tokens, features), jnp.bfloat16),
        in_specs=[
            pl.BlockSpec((tokens, 1), lambda i: (0, 0)),
            pl.BlockSpec((slots, block), lambda i: (0, i)),
            pl.BlockSpec((tokens, block), lambda i: (0, i)),
            pl.BlockSpec((tokens, 1), lambda i: (0, 0)),
        ],
        out_specs=pl.BlockSpec((1, tokens, block), lambda i: (0, 0, i)),
        compiler_params=pltpu.CompilerParams(vmem_limit_bytes=VMEM_BYTES),
        cost_estimate=pl.CostEstimate(
            flops=2 * slots * tokens * features, bytes_accessed=2 * features * (2 * tokens + slots), transcendentals=0
        ),
    )(place, returned, arriving, gate_value)


def local(held, entering, norm_gain, router, w_gate, w_up, w_down, expert_ids):
    experts = router.shape[2]
    group = lax.axis_size("expert")
    panels = group // experts
    tokens, features = entering.shape
    sections = lax.axis_size("section")
    everywhere = ("section", "expert")
    near, mirrored = (lambda x: x ^ 1), (lambda x: panels - 1 - x)
    swap, token_groups = [], []
    for section in range(sections):
        weight_partner, token_partner = (near, mirrored) if section % 2 == 0 else (mirrored, near)
        start = section * group
        for i in range(group):
            swap.append((start + i, start + i - i % panels + weight_partner(i % panels)))
        for x in range(panels):
            if x < token_partner(x):
                pair = (x, token_partner(x))
                token_groups.append([start + e * panels + c for e in range(experts) for c in pair])
    span = 2 * CAP
    slots = experts * span

    gate_other = lax.ppermute(w_gate[0], everywhere, swap)
    up_other = lax.ppermute(w_up[0], everywhere, swap)
    down_other = lax.ppermute(w_down[0], everywhere, swap)
    arrived = passed_along(held[0], "section", 1)

    first = (lax.axis_index("section") == 0).astype(jnp.int32).reshape(1)

    chosen = jnp.pad(expert_ids[0].T.astype(jnp.float32), ((0, 0), (0, features - tokens)))
    small = jnp.concatenate([router[0].T.astype(jnp.float32), norm_gain.astype(jnp.float32), chosen], axis=0)

    def exchange(blocks):
        return lax.all_to_all(
            blocks, everywhere, split_axis=0, concat_axis=0, axis_index_groups=token_groups, tiled=True
        )

    arriving, gate_value, place, sent = front(
        first, small, arrived, jnp.where(first[0] == 1, entering, jnp.zeros_like(entering)), slots
    )
    here = lax.axis_index("section") < sections
    rows = lax.cond(here, exchange, jnp.zeros_like, sent)
    hidden = hidden_units(rows, w_gate[0], w_up[0], gate_other, up_other)
    part = down_part(hidden, w_down[0], down_other)
    return combine(place, exchange(part), arriving, gate_value)


def solution(mesh):
    placed = (
        P("section", "expert", None),
        P("expert", None),
        P("section", None),
        P("section", None, None),
        P("section", None, "expert"),
        P("section", None, "expert"),
        P("section", "expert", None),
        P("section", "expert", None),
    )
    return jax.shard_map(
        local, mesh=mesh, in_specs=placed, out_specs=P("section", "expert", None), check_vma=False
    )
```

```python
import jax
import jax.numpy as jnp
from jax import lax
from jax.experimental import pallas as pl
from jax.experimental.pallas import tpu as pltpu
from jax.sharding import PartitionSpec as P

CAP = 72
VMEM_BYTES = 48 * 1024 * 1024
HIDDEN_VMEM_BYTES = 52 * 1024 * 1024


def passed_along(block, axis, distance):
    devices = range(lax.axis_size(axis))
    route = [(i - distance, i) for i in devices if i - distance in devices]
    return lax.ppermute(block, axis, route)


def product(left, right):
    return jnp.dot(left, right, preferred_element_type=jnp.float32)


def anywhere():
    return pl.BlockSpec(memory_space=pl.ANY)


def column_of(row, zero):
    size = row.shape[1]
    across, down = (lax.broadcasted_iota(jnp.int32, (size, size), d) for d in (1, 0))
    return jnp.sum(jnp.where(across == down, row, zero), axis=1, keepdims=True)


def front_kernel(first_ref, small_ref, arrived_ref, entering_ref, arriving_ref, gate_ref, place_ref, sent_ref, sent, out_sems):
    slots, features = sent.shape
    tokens = arrived_ref.shape[0]
    experts = small_ref.shape[0] - 2
    steps = out_sems.shape[0]
    block = slots // steps
    span = 2 * CAP

    router = small_ref[:experts, :].astype(jnp.bfloat16)
    gain = small_ref[experts : experts + 1, :]
    chosen = small_ref[experts + 1 :, :tokens].astype(jnp.int32)
    assigned = chosen == lax.broadcasted_iota(jnp.int32, (experts, tokens), 0)
    across, down = (lax.broadcasted_iota(jnp.int32, (tokens, tokens), d) for d in (1, 0))
    ranks = product(assigned.astype(jnp.bfloat16), (down < across).astype(jnp.bfloat16))
    rank = jnp.sum(jnp.where(assigned, ranks, 0.0), axis=0, keepdims=True).astype(jnp.int32)
    place = rank + chosen * span
    place_ref[...] = column_of(place, 0)
    slot = lax.broadcasted_iota(jnp.int32, (slots, tokens), 0)
    row_slot = jnp.where(slot % span < CAP, slot, slot - CAP)
    select = (place == row_slot).astype(jnp.bfloat16)

    arriving = jnp.where(first_ref[0] == 1, entering_ref[...], arrived_ref[...])
    arriving_ref[...] = arriving
    values = arriving.astype(jnp.float32)
    written = []
    scaling = lax.rsqrt(jnp.mean(values * values, axis=-1, keepdims=True) + 1e-06)
    normed = (values * scaling * gain).astype(jnp.bfloat16)
    for step in range(steps):
        here = pl.ds(step * block, block)
        sent[here, :] = product(select[step * block : (step + 1) * block], normed).astype(jnp.bfloat16)
        copy = pltpu.make_async_copy(sent.at[here], sent_ref.at[here], out_sems.at[step])
        copy.start()
        written.append(copy)
    logits = lax.dot_general(router, normed, (((1,), (1,)), ((), ())), preferred_element_type=jnp.float32)
    weights = jnp.exp(logits)
    probability = weights / jnp.sum(weights, axis=0, keepdims=True)
    gate_ref[...] = column_of(jnp.sum(jnp.where(assigned, probability, 0.0), axis=0, keepdims=True), 0.0)
    for copy in written:
        copy.wait()


def front(first, small, arrived, entering, slots, steps=4):
    tokens, features = entering.shape
    vmem = pl.BlockSpec(memory_space=pltpu.VMEM)
    return pl.pallas_call(
        front_kernel,
        out_shape=(
            jax.ShapeDtypeStruct((tokens, features), jnp.bfloat16),
            jax.ShapeDtypeStruct((tokens, 1), jnp.float32),
            jax.ShapeDtypeStruct((tokens, 1), jnp.int32),
            jax.ShapeDtypeStruct((slots, features), jnp.bfloat16),
        ),
        in_specs=[pl.BlockSpec(memory_space=pltpu.SMEM)] + [vmem] * 3,
        out_specs=(vmem, vmem, vmem, anywhere()),
        scratch_shapes=[
            pltpu.VMEM((slots, features), jnp.bfloat16),
            pltpu.SemaphoreType.DMA((steps,)),
        ],
        compiler_params=pltpu.CompilerParams(vmem_limit_bytes=VMEM_BYTES),
        cost_estimate=pl.CostEstimate(
            flops=40 * slots * tokens * features, bytes_accessed=2 * features * (3 * tokens + slots), transcendentals=tokens
        ),
    )(first, small, arrived, entering)


def hidden_kernel(rows_ref, gate_ref, up_ref, gate_other_ref, up_other_ref, hidden_ref, rows, gate_up, in_sems):
    count, features = rows.shape
    units = gate_ref.shape[1]
    steps = in_sems.shape[0] - 4
    block = count // steps

    def fetch(source, target, index):
        copy = pltpu.make_async_copy(source, target, in_sems.at[index])
        copy.start()
        return copy

    first, second = pl.ds(0, units), pl.ds(units, units)
    blocks = [pl.ds(step * block, block) for step in range(steps)]
    row_copies = [fetch(rows_ref.at[blocks[0]], rows.at[blocks[0]], 4)]
    panels = [(fetch(gate_ref, gate_up.at[0, :, first], 0), fetch(up_ref, gate_up.at[0, :, second], 1))]
    row_copies += [fetch(rows_ref.at[blocks[i]], rows.at[blocks[i]], 4 + i) for i in range(1, steps)]
    panels += [(fetch(gate_other_ref, gate_up.at[1, :, first], 2), fetch(up_other_ref, gate_up.at[1, :, second], 3))]
    for i, copies in enumerate(panels):
        for copy in copies:
            copy.wait()
        for step, here in enumerate(blocks):
            if i == 0:
                row_copies[step].wait()
            both = product(rows[here, :], gate_up[i])
            units_here = jax.nn.silu(both[:, :units]) * both[:, units:]
            hidden_ref[here, i * units : (i + 1) * units] = units_here.astype(jnp.bfloat16)


def hidden_units(rows, gate, up, gate_other, up_other, steps=2):
    count, features = rows.shape
    units = gate.shape[1]
    return pl.pallas_call(
        hidden_kernel,
        out_shape=jax.ShapeDtypeStruct((count, 2 * units), jnp.bfloat16),
        in_specs=[anywhere()] * 5,
        out_specs=pl.BlockSpec(memory_space=pltpu.VMEM),
        scratch_shapes=[
            pltpu.VMEM((count, features), jnp.bfloat16),
            pltpu.VMEM((2, features, 2 * units), jnp.bfloat16),
            pltpu.SemaphoreType.DMA((4 + steps,)),
        ],
        compiler_params=pltpu.CompilerParams(vmem_limit_bytes=HIDDEN_VMEM_BYTES),
        cost_estimate=pl.CostEstimate(
            flops=8 * count * features * units,
            bytes_accessed=2 * (count * features + 4 * features * units),
            transcendentals=2 * count * units,
        ),
    )(rows, gate, up, gate_other, up_other)


def down_kernel(hidden_ref, down_ref, down_other_ref, part_ref):
    units = down_ref.shape[0]
    total = product(hidden_ref[:, :units], down_ref[...])
    total += product(hidden_ref[:, units:], down_other_ref[...])
    part_ref[...] = total.astype(part_ref.dtype)


def down_part(hidden, down, down_other, steps=2):
    count = hidden.shape[0]
    units, features = down.shape
    block = features // steps
    return pl.pallas_call(
        down_kernel,
        grid=(steps,),
        out_shape=jax.ShapeDtypeStruct((count, features), jnp.bfloat16),
        in_specs=[
            pl.BlockSpec((count, 2 * units), lambda i: (0, 0)),
            pl.BlockSpec((units, block), lambda i: (0, i)),
            pl.BlockSpec((units, block), lambda i: (0, i)),
        ],
        out_specs=pl.BlockSpec((count, block), lambda i: (0, i)),
        compiler_params=pltpu.CompilerParams(vmem_limit_bytes=VMEM_BYTES),
        cost_estimate=pl.CostEstimate(
            flops=4 * count * features * units,
            bytes_accessed=2 * (count * (features + 2 * units) + 2 * features * units),
            transcendentals=0,
        ),
    )(hidden, down, down_other)


def combine_kernel(place_ref, returned_ref, arriving_ref, gate_ref, mixed_ref):
    tokens, slots = place_ref.shape[0], returned_ref.shape[0]
    slot = lax.broadcasted_iota(jnp.int32, (tokens, slots), 1)
    row_slot = jnp.where(slot % (2 * CAP) < CAP, slot, slot - CAP)
    spread = (place_ref[...] == row_slot).astype(jnp.bfloat16)
    mixture = product(spread, returned_ref[...])
    mixed = arriving_ref[...].astype(jnp.float32) + gate_ref[...] * mixture
    mixed_ref[0] = mixed.astype(mixed_ref.dtype)


def combine(place, returned, arriving, gate_value, steps=1):
    tokens, features = arriving.shape
    slots = returned.shape[0]
    block = features // steps
    return pl.pallas_call(
        combine_kernel,
        grid=(steps,),
        out_shape=jax.ShapeDtypeStruct((1, tokens, features), jnp.bfloat16),
        in_specs=[
            pl.BlockSpec((tokens, 1), lambda i: (0, 0)),
            pl.BlockSpec((slots, block), lambda i: (0, i)),
            pl.BlockSpec((tokens, block), lambda i: (0, i)),
            pl.BlockSpec((tokens, 1), lambda i: (0, 0)),
        ],
        out_specs=pl.BlockSpec((1, tokens, block), lambda i: (0, 0, i)),
        compiler_params=pltpu.CompilerParams(vmem_limit_bytes=VMEM_BYTES),
        cost_estimate=pl.CostEstimate(
            flops=2 * slots * tokens * features, bytes_accessed=2 * features * (2 * tokens + slots), transcendentals=0
        ),
    )(place, returned, arriving, gate_value)


def local(held, entering, norm_gain, router, w_gate, w_up, w_down, expert_ids):
    experts = router.shape[2]
    group = lax.axis_size("expert")
    panels = group // experts
    tokens, features = entering.shape
    sections = lax.axis_size("section")
    everywhere = ("section", "expert")
    near, mirrored = (lambda x: x ^ 1), (lambda x: panels - 1 - x)
    swap, token_groups = [], []
    for section in range(sections):
        weight_partner, token_partner = (near, mirrored) if section % 2 == 0 else (mirrored, near)
        start = section * group
        for i in range(group):
            swap.append((start + i, start + i - i % panels + weight_partner(i % panels)))
        for x in range(panels):
            if x < token_partner(x):
                pair = (x, token_partner(x))
                token_groups.append([start + e * panels + c for e in range(experts) for c in pair])
    span = 2 * CAP
    slots = experts * span

    gate_other = lax.ppermute(w_gate[0], everywhere, swap)
    up_other = lax.ppermute(w_up[0], everywhere, swap)
    down_other = lax.ppermute(w_down[0], everywhere, swap)
    arrived = passed_along(held[0], "section", 1)

    first = (lax.axis_index("section") == 0).astype(jnp.int32).reshape(1)

    chosen = jnp.pad(expert_ids[0].T.astype(jnp.float32), ((0, 0), (0, features - tokens)))
    small = jnp.concatenate([router[0].T.astype(jnp.float32), norm_gain.astype(jnp.float32), chosen], axis=0)

    def exchange(blocks):
        return lax.all_to_all(
            blocks, everywhere, split_axis=0, concat_axis=0, axis_index_groups=token_groups, tiled=True
        )

    arriving, gate_value, place, sent = front(
        first, small, arrived, jnp.where(first[0] == 1, entering, jnp.zeros_like(entering)), slots
    )
    here = lax.axis_index("section") < sections
    rows = lax.cond(here, exchange, jnp.zeros_like, sent)
    hidden = hidden_units(rows, w_gate[0], w_up[0], gate_other, up_other)
    part = down_part(hidden, w_down[0], down_other)
    return combine(place, exchange(part), arriving, gate_value)


def solution(mesh):
    placed = (
        P("section", "expert", None),
        P("expert", None),
        P("section", None),
        P("section", None, None),
        P("section", None, "expert"),
        P("section", None, "expert"),
        P("section", "expert", None),
        P("section", "expert", None),
    )
    return jax.shard_map(
        local, mesh=mesh, in_specs=placed, out_specs=P("section", "expert", None), check_vma=False
    )
```

```python
import jax
import jax.numpy as jnp
from jax import lax
from jax.experimental import pallas as pl
from jax.experimental.pallas import tpu as pltpu
from jax.sharding import PartitionSpec as P

CAP = 72
VMEM_BYTES = 48 * 1024 * 1024
HIDDEN_VMEM_BYTES = 52 * 1024 * 1024


def passed_along(block, axis, distance):
    devices = range(lax.axis_size(axis))
    route = [(i - distance, i) for i in devices if i - distance in devices]
    return lax.ppermute(block, axis, route)


def product(left, right):
    return jnp.dot(left, right, preferred_element_type=jnp.float32)


def anywhere():
    return pl.BlockSpec(memory_space=pl.ANY)


def column_of(row, zero):
    size = row.shape[1]
    across, down = (lax.broadcasted_iota(jnp.int32, (size, size), d) for d in (1, 0))
    return jnp.sum(jnp.where(across == down, row, zero), axis=1, keepdims=True)


def front_kernel(first_ref, small_ref, arrived_ref, entering_ref, arriving_ref, gate_ref, place_ref, sent_ref, sent, out_sems):
    slots, features = sent.shape
    tokens = arrived_ref.shape[0]
    experts = small_ref.shape[0] - 2
    steps = out_sems.shape[0]
    block = slots // steps
    span = 2 * CAP

    router = small_ref[:experts, :].astype(jnp.bfloat16)
    gain = small_ref[experts : experts + 1, :]
    chosen = small_ref[experts + 1 :, :tokens].astype(jnp.int32)
    assigned = chosen == lax.broadcasted_iota(jnp.int32, (experts, tokens), 0)
    across, down = (lax.broadcasted_iota(jnp.int32, (tokens, tokens), d) for d in (1, 0))
    ranks = product(assigned.astype(jnp.bfloat16), (down < across).astype(jnp.bfloat16))
    rank = jnp.sum(jnp.where(assigned, ranks, 0.0), axis=0, keepdims=True).astype(jnp.int32)
    place = rank + chosen * span
    place_ref[...] = column_of(place, 0)
    slot = lax.broadcasted_iota(jnp.int32, (slots, tokens), 0)
    row_slot = jnp.where(slot % span < CAP, slot, slot - CAP)
    select = (place == row_slot).astype(jnp.bfloat16)

    arriving = jnp.where(first_ref[0] == 1, entering_ref[...], arrived_ref[...])
    arriving_ref[...] = arriving
    values = arriving.astype(jnp.float32)
    written = []
    scaling = lax.rsqrt(jnp.mean(values * values, axis=-1, keepdims=True) + 1e-06)
    normed = (values * scaling * gain).astype(jnp.bfloat16)
    for step in range(steps):
        here = pl.ds(step * block, block)
        sent[here, :] = product(select[step * block : (step + 1) * block], normed).astype(jnp.bfloat16)
        copy = pltpu.make_async_copy(sent.at[here], sent_ref.at[here], out_sems.at[step])
        copy.start()
        written.append(copy)
    logits = lax.dot_general(router, normed, (((1,), (1,)), ((), ())), preferred_element_type=jnp.float32)
    weights = jnp.exp(logits)
    probability = weights / jnp.sum(weights, axis=0, keepdims=True)
    gate_ref[...] = column_of(jnp.sum(jnp.where(assigned, probability, 0.0), axis=0, keepdims=True), 0.0)
    for copy in written:
        copy.wait()


def front(first, small, arrived, entering, slots, steps=4):
    tokens, features = entering.shape
    vmem = pl.BlockSpec(memory_space=pltpu.VMEM)
    return pl.pallas_call(
        front_kernel,
        out_shape=(
            jax.ShapeDtypeStruct((tokens, features), jnp.bfloat16),
            jax.ShapeDtypeStruct((tokens, 1), jnp.float32),
            jax.ShapeDtypeStruct((tokens, 1), jnp.int32),
            jax.ShapeDtypeStruct((slots, features), jnp.bfloat16),
        ),
        in_specs=[pl.BlockSpec(memory_space=pltpu.SMEM)] + [vmem] * 3,
        out_specs=(vmem, vmem, vmem, anywhere()),
        scratch_shapes=[
            pltpu.VMEM((slots, features), jnp.bfloat16),
            pltpu.SemaphoreType.DMA((steps,)),
        ],
        compiler_params=pltpu.CompilerParams(vmem_limit_bytes=VMEM_BYTES),
        cost_estimate=pl.CostEstimate(
            flops=40 * slots * tokens * features, bytes_accessed=2 * features * (3 * tokens + slots), transcendentals=tokens
        ),
    )(first, small, arrived, entering)


def hidden_kernel(rows_ref, gate_ref, up_ref, gate_other_ref, up_other_ref, hidden_ref, rows, gate_up, in_sems):
    count, features = rows.shape
    units = gate_ref.shape[1]
    steps = in_sems.shape[0] - 4
    block = count // steps

    def fetch(source, target, index):
        copy = pltpu.make_async_copy(source, target, in_sems.at[index])
        copy.start()
        return copy

    first, second = pl.ds(0, units), pl.ds(units, units)
    blocks = [pl.ds(step * block, block) for step in range(steps)]
    row_copies = [fetch(rows_ref.at[blocks[0]], rows.at[blocks[0]], 4)]
    panels = [(fetch(gate_ref, gate_up.at[0, :, first], 0), fetch(up_ref, gate_up.at[0, :, second], 1))]
    row_copies += [fetch(rows_ref.at[blocks[i]], rows.at[blocks[i]], 4 + i) for i in range(1, steps)]
    panels += [(fetch(gate_other_ref, gate_up.at[1, :, first], 2), fetch(up_other_ref, gate_up.at[1, :, second], 3))]
    for i, copies in enumerate(panels):
        for copy in copies:
            copy.wait()
        for step, here in enumerate(blocks):
            if i == 0:
                row_copies[step].wait()
            both = product(rows[here, :], gate_up[i])
            units_here = jax.nn.silu(both[:, :units]) * both[:, units:]
            hidden_ref[here, i * units : (i + 1) * units] = units_here.astype(jnp.bfloat16)


def hidden_units(rows, gate, up, gate_other, up_other, steps=2):
    count, features = rows.shape
    units = gate.shape[1]
    return pl.pallas_call(
        hidden_kernel,
        out_shape=jax.ShapeDtypeStruct((count, 2 * units), jnp.bfloat16),
        in_specs=[anywhere()] * 5,
        out_specs=pl.BlockSpec(memory_space=pltpu.VMEM),
        scratch_shapes=[
            pltpu.VMEM((count, features), jnp.bfloat16),
            pltpu.VMEM((2, features, 2 * units), jnp.bfloat16),
            pltpu.SemaphoreType.DMA((4 + steps,)),
        ],
        compiler_params=pltpu.CompilerParams(vmem_limit_bytes=HIDDEN_VMEM_BYTES),
        cost_estimate=pl.CostEstimate(
            flops=8 * count * features * units,
            bytes_accessed=2 * (count * features + 4 * features * units),
            transcendentals=2 * count * units,
        ),
    )(rows, gate, up, gate_other, up_other)


def down_kernel(hidden_ref, down_ref, down_other_ref, part_ref):
    units = down_ref.shape[0]
    total = product(hidden_ref[:, :units], down_ref[...])
    total += product(hidden_ref[:, units:], down_other_ref[...])
    part_ref[...] = total.astype(part_ref.dtype)


def down_part(hidden, down, down_other, steps=2):
    count = hidden.shape[0]
    units, features = down.shape
    block = features // steps
    return pl.pallas_call(
        down_kernel,
        grid=(steps,),
        out_shape=jax.ShapeDtypeStruct((count, features), jnp.bfloat16),
        in_specs=[
            pl.BlockSpec((count, 2 * units), lambda i: (0, 0)),
            pl.BlockSpec((units, block), lambda i: (0, i)),
            pl.BlockSpec((units, block), lambda i: (0, i)),
        ],
        out_specs=pl.BlockSpec((count, block), lambda i: (0, i)),
        compiler_params=pltpu.CompilerParams(vmem_limit_bytes=VMEM_BYTES),
        cost_estimate=pl.CostEstimate(
            flops=4 * count * features * units,
            bytes_accessed=2 * (count * (features + 2 * units) + 2 * features * units),
            transcendentals=0,
        ),
    )(hidden, down, down_other)


def combine_kernel(place_ref, returned_ref, arriving_ref, gate_ref, mixed_ref):
    tokens, slots = place_ref.shape[0], returned_ref.shape[0]
    slot = lax.broadcasted_iota(jnp.int32, (tokens, slots), 1)
    row_slot = jnp.where(slot % (2 * CAP) < CAP, slot, slot - CAP)
    spread = (place_ref[...] == row_slot).astype(jnp.bfloat16)
    mixture = product(spread, returned_ref[...])
    mixed = arriving_ref[...].astype(jnp.float32) + gate_ref[...] * mixture
    mixed_ref[0] = mixed.astype(mixed_ref.dtype)


def combine(place, returned, arriving, gate_value, steps=1):
    tokens, features = arriving.shape
    slots = returned.shape[0]
    block = features // steps
    return pl.pallas_call(
        combine_kernel,
        grid=(steps,),
        out_shape=jax.ShapeDtypeStruct((1, tokens, features), jnp.bfloat16),
        in_specs=[
            pl.BlockSpec((tokens, 1), lambda i: (0, 0)),
            pl.BlockSpec((slots, block), lambda i: (0, i)),
            pl.BlockSpec((tokens, block), lambda i: (0, i)),
            pl.BlockSpec((tokens, 1), lambda i: (0, 0)),
        ],
        out_specs=pl.BlockSpec((1, tokens, block), lambda i: (0, 0, i)),
        compiler_params=pltpu.CompilerParams(vmem_limit_bytes=VMEM_BYTES),
        cost_estimate=pl.CostEstimate(
            flops=2 * slots * tokens * features, bytes_accessed=2 * features * (2 * tokens + slots), transcendentals=0
        ),
    )(place, returned, arriving, gate_value)


def local(held, entering, norm_gain, router, w_gate, w_up, w_down, expert_ids):
    experts = router.shape[2]
    group = lax.axis_size("expert")
    panels = group // experts
    tokens, features = entering.shape
    sections = lax.axis_size("section")
    everywhere = ("section", "expert")
    near, mirrored = (lambda x: x ^ 1), (lambda x: panels - 1 - x)
    swap, token_groups = [], []
    for section in range(sections):
        weight_partner, token_partner = (near, mirrored) if section % 2 == 0 else (mirrored, near)
        start = section * group
        for i in range(group):
            swap.append((start + i, start + i - i % panels + weight_partner(i % panels)))
        for x in range(panels):
            if x < token_partner(x):
                pair = (x, token_partner(x))
                token_groups.append([start + e * panels + c for e in range(experts) for c in pair])
    span = 2 * CAP
    slots = experts * span

    gate_other = lax.ppermute(w_gate[0], everywhere, swap)
    up_other = lax.ppermute(w_up[0], everywhere, swap)
    down_other = lax.ppermute(w_down[0], everywhere, swap)
    arrived = passed_along(held[0], "section", 1)

    first = (lax.axis_index("section") == 0).astype(jnp.int32).reshape(1)

    numbers = jnp.pad(expert_ids[0].T, ((experts + 1, 0), (0, features - tokens)))
    small = jnp.pad(router[0].T, ((0, 2), (0, 0))) + jnp.pad(norm_gain, ((experts, 1), (0, 0)))
    small = small.astype(jnp.float32) + numbers.astype(jnp.float32)

    def exchange(blocks):
        return lax.all_to_all(
            blocks, everywhere, split_axis=0, concat_axis=0, axis_index_groups=token_groups, tiled=True
        )

    arriving, gate_value, place, sent = front(
        first, small, arrived, jnp.where(first[0] == 1, entering, jnp.zeros_like(entering)), slots
    )
    here = lax.axis_index("section") < sections
    rows = lax.cond(here, exchange, jnp.zeros_like, sent)
    hidden = hidden_units(rows, w_gate[0], w_up[0], gate_other, up_other)
    part = down_part(hidden, w_down[0], down_other)
    return combine(place, exchange(part), arriving, gate_value)


def solution(mesh):
    placed = (
        P("section", "expert", None),
        P("expert", None),
        P("section", None),
        P("section", None, None),
        P("section", None, "expert"),
        P("section", None, "expert"),
        P("section", "expert", None),
        P("section", "expert", None),
    )
    return jax.shard_map(
        local, mesh=mesh, in_specs=placed, out_specs=P("section", "expert", None), check_vma=False
    )
```

```python
import jax
import jax.numpy as jnp
from jax import lax
from jax.experimental import pallas as pl
from jax.experimental.pallas import tpu as pltpu
from jax.sharding import PartitionSpec as P

CAP = 72
VMEM_BYTES = 48 * 1024 * 1024
HIDDEN_VMEM_BYTES = 52 * 1024 * 1024


def passed_along(block, axis, distance):
    devices = range(lax.axis_size(axis))
    route = [(i - distance, i) for i in devices if i - distance in devices]
    return lax.ppermute(block, axis, route)


def product(left, right):
    return jnp.dot(left, right, preferred_element_type=jnp.float32)


def anywhere():
    return pl.BlockSpec(memory_space=pl.ANY)


def column_of(row, zero):
    size = row.shape[1]
    across, down = (lax.broadcasted_iota(jnp.int32, (size, size), d) for d in (1, 0))
    return jnp.sum(jnp.where(across == down, row, zero), axis=1, keepdims=True)


def front_kernel(first_ref, small_ref, arrived_ref, entering_ref, arriving_ref, gate_ref, place_ref, sent_ref, sent, out_sems):
    slots, features = sent.shape
    tokens = arrived_ref.shape[0]
    experts = small_ref.shape[0] - 2
    steps = out_sems.shape[0]
    block = slots // steps
    span = 2 * CAP

    router = small_ref[:experts, :].astype(jnp.bfloat16)
    gain = small_ref[experts : experts + 1, :]
    chosen = small_ref[experts + 1 :, :tokens].astype(jnp.int32)
    assigned = chosen == lax.broadcasted_iota(jnp.int32, (experts, tokens), 0)
    across, down = (lax.broadcasted_iota(jnp.int32, (tokens, tokens), d) for d in (1, 0))
    ranks = product(assigned.astype(jnp.bfloat16), (down < across).astype(jnp.bfloat16))
    rank = jnp.sum(jnp.where(assigned, ranks, 0.0), axis=0, keepdims=True).astype(jnp.int32)
    place = rank + chosen * span
    place_ref[...] = column_of(place, 0)
    slot = lax.broadcasted_iota(jnp.int32, (slots, tokens), 0)
    row_slot = jnp.where(slot % span < CAP, slot, slot - CAP)
    select = (place == row_slot).astype(jnp.bfloat16)

    arriving = jnp.where(first_ref[0] == 1, entering_ref[...], arrived_ref[...])
    arriving_ref[...] = arriving
    values = arriving.astype(jnp.float32)
    written = []
    scaling = lax.rsqrt(jnp.mean(values * values, axis=-1, keepdims=True) + 1e-06)
    normed = (values * scaling * gain).astype(jnp.bfloat16)
    for step in range(steps):
        here = pl.ds(step * block, block)
        sent[here, :] = product(select[step * block : (step + 1) * block], normed).astype(jnp.bfloat16)
        copy = pltpu.make_async_copy(sent.at[here], sent_ref.at[here], out_sems.at[step])
        copy.start()
        written.append(copy)
    logits = lax.dot_general(router, normed, (((1,), (1,)), ((), ())), preferred_element_type=jnp.float32)
    weights = jnp.exp(logits)
    probability = weights / jnp.sum(weights, axis=0, keepdims=True)
    gate_ref[...] = column_of(jnp.sum(jnp.where(assigned, probability, 0.0), axis=0, keepdims=True), 0.0)
    for copy in written:
        copy.wait()


def front(first, small, arrived, entering, slots, steps=4):
    tokens, features = entering.shape
    vmem = pl.BlockSpec(memory_space=pltpu.VMEM)
    return pl.pallas_call(
        front_kernel,
        out_shape=(
            jax.ShapeDtypeStruct((tokens, features), jnp.bfloat16),
            jax.ShapeDtypeStruct((tokens, 1), jnp.float32),
            jax.ShapeDtypeStruct((tokens, 1), jnp.int32),
            jax.ShapeDtypeStruct((slots, features), jnp.bfloat16),
        ),
        in_specs=[pl.BlockSpec(memory_space=pltpu.SMEM)] + [vmem] * 3,
        out_specs=(vmem, vmem, vmem, anywhere()),
        scratch_shapes=[
            pltpu.VMEM((slots, features), jnp.bfloat16),
            pltpu.SemaphoreType.DMA((steps,)),
        ],
        compiler_params=pltpu.CompilerParams(vmem_limit_bytes=VMEM_BYTES),
        cost_estimate=pl.CostEstimate(
            flops=40 * slots * tokens * features, bytes_accessed=2 * features * (3 * tokens + slots), transcendentals=tokens
        ),
    )(first, small, arrived, entering)


def hidden_kernel(rows_ref, gate_ref, up_ref, gate_other_ref, up_other_ref, down_ref, hidden_ref, own_ref, rows, gate_up, down, in_sems):
    count, features = rows.shape
    units = gate_ref.shape[1]
    steps = in_sems.shape[0] - 5
    block = count // steps

    def fetch(source, target, index):
        copy = pltpu.make_async_copy(source, target, in_sems.at[index])
        copy.start()
        return copy

    first, second = pl.ds(0, units), pl.ds(units, units)
    blocks = [pl.ds(step * block, block) for step in range(steps)]
    row_copies = [fetch(rows_ref.at[blocks[0]], rows.at[blocks[0]], 4)]
    panels = [(fetch(gate_ref, gate_up.at[0, :, first], 0), fetch(up_ref, gate_up.at[0, :, second], 1))]
    row_copies += [fetch(rows_ref.at[blocks[i]], rows.at[blocks[i]], 4 + i) for i in range(1, steps)]
    panels += [(fetch(gate_other_ref, gate_up.at[1, :, first], 2), fetch(up_other_ref, gate_up.at[1, :, second], 3))]
    down_copy = fetch(down_ref, down, 4 + steps)
    for i, copies in enumerate(panels):
        for copy in copies:
            copy.wait()
        for step, here in enumerate(blocks):
            if i == 0:
                row_copies[step].wait()
            both = product(rows[here, :], gate_up[i])
            units_here = jax.nn.silu(both[:, :units]) * both[:, units:]
            hidden = units_here.astype(jnp.bfloat16)
            if i == 0:
                if step == 0:
                    down_copy.wait()
                own_ref[here, :] = product(hidden, down[...])
            else:
                hidden_ref[here, :] = hidden


def hidden_units(rows, gate, up, gate_other, up_other, down, steps=2):
    count, features = rows.shape
    units = gate.shape[1]
    return pl.pallas_call(
        hidden_kernel,
        out_shape=(
            jax.ShapeDtypeStruct((count, units), jnp.bfloat16),
            jax.ShapeDtypeStruct((count, features), jnp.float32),
        ),
        in_specs=[anywhere()] * 6,
        out_specs=(pl.BlockSpec(memory_space=pltpu.VMEM), pl.BlockSpec(memory_space=pltpu.VMEM)),
        scratch_shapes=[
            pltpu.VMEM((count, features), jnp.bfloat16),
            pltpu.VMEM((2, features, 2 * units), jnp.bfloat16),
            pltpu.VMEM((units, features), jnp.bfloat16),
            pltpu.SemaphoreType.DMA((5 + steps,)),
        ],
        compiler_params=pltpu.CompilerParams(vmem_limit_bytes=HIDDEN_VMEM_BYTES),
        cost_estimate=pl.CostEstimate(
            flops=8 * count * features * units,
            bytes_accessed=2 * (count * features + 4 * features * units),
            transcendentals=2 * count * units,
        ),
    )(rows, gate, up, gate_other, up_other, down)


def down_kernel(own_ref, hidden_ref, down_ref, part_ref):
    total = own_ref[...] + product(hidden_ref[...], down_ref[...])
    part_ref[...] = total.astype(part_ref.dtype)


def down_part(own, hidden, down_other, steps=2):
    count, units = hidden.shape
    features = down_other.shape[1]
    block = features // steps
    return pl.pallas_call(
        down_kernel,
        grid=(steps,),
        out_shape=jax.ShapeDtypeStruct((count, features), jnp.bfloat16),
        in_specs=[
            pl.BlockSpec((count, block), lambda i: (0, i)),
            pl.BlockSpec((count, units), lambda i: (0, 0)),
            pl.BlockSpec((units, block), lambda i: (0, i)),
        ],
        out_specs=pl.BlockSpec((count, block), lambda i: (0, i)),
        compiler_params=pltpu.CompilerParams(vmem_limit_bytes=VMEM_BYTES),
        cost_estimate=pl.CostEstimate(
            flops=2 * count * features * units,
            bytes_accessed=6 * count * features + 2 * units * (count + features),
            transcendentals=0,
        ),
    )(own, hidden, down_other)


def combine_kernel(place_ref, returned_ref, arriving_ref, gate_ref, mixed_ref):
    tokens, slots = place_ref.shape[0], returned_ref.shape[0]
    slot = lax.broadcasted_iota(jnp.int32, (tokens, slots), 1)
    row_slot = jnp.where(slot % (2 * CAP) < CAP, slot, slot - CAP)
    spread = (place_ref[...] == row_slot).astype(jnp.bfloat16)
    mixture = product(spread, returned_ref[...])
    mixed = arriving_ref[...].astype(jnp.float32) + gate_ref[...] * mixture
    mixed_ref[0] = mixed.astype(mixed_ref.dtype)


def combine(place, returned, arriving, gate_value, steps=1):
    tokens, features = arriving.shape
    slots = returned.shape[0]
    block = features // steps
    return pl.pallas_call(
        combine_kernel,
        grid=(steps,),
        out_shape=jax.ShapeDtypeStruct((1, tokens, features), jnp.bfloat16),
        in_specs=[
            pl.BlockSpec((tokens, 1), lambda i: (0, 0)),
            pl.BlockSpec((slots, block), lambda i: (0, i)),
            pl.BlockSpec((tokens, block), lambda i: (0, i)),
            pl.BlockSpec((tokens, 1), lambda i: (0, 0)),
        ],
        out_specs=pl.BlockSpec((1, tokens, block), lambda i: (0, 0, i)),
        compiler_params=pltpu.CompilerParams(vmem_limit_bytes=VMEM_BYTES),
        cost_estimate=pl.CostEstimate(
            flops=2 * slots * tokens * features, bytes_accessed=2 * features * (2 * tokens + slots), transcendentals=0
        ),
    )(place, returned, arriving, gate_value)


def local(held, entering, norm_gain, router, w_gate, w_up, w_down, expert_ids):
    experts = router.shape[2]
    group = lax.axis_size("expert")
    panels = group // experts
    tokens, features = entering.shape
    sections = lax.axis_size("section")
    everywhere = ("section", "expert")
    near, mirrored = (lambda x: x ^ 1), (lambda x: panels - 1 - x)
    swap, token_groups = [], []
    for section in range(sections):
        weight_partner, token_partner = (near, mirrored) if section % 2 == 0 else (mirrored, near)
        start = section * group
        for i in range(group):
            swap.append((start + i, start + i - i % panels + weight_partner(i % panels)))
        for x in range(panels):
            if x < token_partner(x):
                pair = (x, token_partner(x))
                token_groups.append([start + e * panels + c for e in range(experts) for c in pair])
    span = 2 * CAP
    slots = experts * span

    gate_other = lax.ppermute(w_gate[0], everywhere, swap)
    up_other = lax.ppermute(w_up[0], everywhere, swap)
    down_other = lax.ppermute(w_down[0], everywhere, swap)
    arrived = passed_along(held[0], "section", 1)

    first = (lax.axis_index("section") == 0).astype(jnp.int32).reshape(1)

    numbers = jnp.pad(expert_ids[0].T, ((experts + 1, 0), (0, features - tokens)))
    small = jnp.pad(router[0].T, ((0, 2), (0, 0))) + jnp.pad(norm_gain, ((experts, 1), (0, 0)))
    small = small.astype(jnp.float32) + numbers.astype(jnp.float32)

    def exchange(blocks):
        return lax.all_to_all(
            blocks, everywhere, split_axis=0, concat_axis=0, axis_index_groups=token_groups, tiled=True
        )

    arriving, gate_value, place, sent = front(
        first, small, arrived, jnp.where(first[0] == 1, entering, jnp.zeros_like(entering)), slots
    )
    here = lax.axis_index("section") < sections
    rows = lax.cond(here, exchange, jnp.zeros_like, sent)
    hidden, own = hidden_units(rows, w_gate[0], w_up[0], gate_other, up_other, w_down[0])
    part = down_part(own, hidden, down_other)
    return combine(place, exchange(part), arriving, gate_value)


def solution(mesh):
    placed = (
        P("section", "expert", None),
        P("expert", None),
        P("section", None),
        P("section", None, None),
        P("section", None, "expert"),
        P("section", None, "expert"),
        P("section", "expert", None),
        P("section", "expert", None),
    )
    return jax.shard_map(
        local, mesh=mesh, in_specs=placed, out_specs=P("section", "expert", None), check_vma=False
    )
```
